32 devices in a mesh: chan: 4 (over y, x), tm: 8 (over z, core).
Axes of the slice: x: 2, y: 2, z: 4, core: 2. Of those that a mesh axis runs over, the one named last changes fastest.
Arguments:
- records: bfloat16 [352, 512, 1024], P('tm', 'chan'), may hold values from -2000 to 2000, as said below
Outputs:
- cross_near: float32 [32, 2, 2, 512, 2, 128], P('tm', None, None, 'chan')
- cross_far: float32 [32, 512, 2, 128], P('tm', 'chan')
The draws below stay inside these ranges and needn't reach their ends.
Inputs may be any that keep to these rules, and one draw needn't show every extreme that they name: Raw strain-rate records.
All inputs are finite; a program needn't handle non-finite values.
Results may differ from the reference program's by a relative error of at most 0.009.
Values may be sent and summed in bfloat16 or wider, within the bound.
No kernel may reach another device: no remote copies, remote signals or barrier semaphores. Data moves between devices by JAX's collectives and lax.ppermute only.
A program may use at most 128 MiB of HBM per device.

```python
import math
import jax
import jax.numpy as jnp
from jax import lax

CH_DEV = 128
CHANNELS = 512
FREQS = 64
SAMPLES = 1024
FIRST_BIN = 32
W_DEV = 44
WINDOWS = 352
HALF = 2
N_TM = 8


def draw_records(key, part):
    noise_key = jax.random.fold_in(key, 11)
    channel_key = jax.random.fold_in(key, 12)
    window_key = jax.random.fold_in(key, 13)
    channel_scale = jnp.exp(jax.random.uniform(channel_key, (1, CHANNELS, 1), jnp.float32, 0.0, math.log(10.0)))
    window_scale = jnp.exp(jax.random.uniform(window_key, (WINDOWS, 1, 1), jnp.float32, 0.0, math.log(10.0)))
    base = jax.random.normal(noise_key, (WINDOWS, CHANNELS, SAMPLES), jnp.float32)
    base = jnp.clip(base, -6.0, 6.0)
    return (base * channel_scale * window_scale).astype(jnp.bfloat16)


def setup_inputs(seed: int = 0) -> dict:
    key_of = jax.random.split(jax.random.key(seed), 2)
    records = draw_records(jax.random.fold_in(key_of[1], 71), 0)
    return {"records": records}


EPSILON = 1e-06

def dft_table(sample_count, frequency_count, first_bin):
    positions = jnp.arange(sample_count, dtype=jnp.int32)
    bin_numbers = jnp.arange(frequency_count, dtype=jnp.int32) + first_bin
    phase_index = bin_numbers[:, None] * positions[None, :] % sample_count
    phase_angle = 2.0 * math.pi / sample_count * phase_index.astype(jnp.float32)
    hann_taper = 0.5 - 0.5 * jnp.cos(2.0 * math.pi / sample_count * positions.astype(jnp.float32))
    cosine = hann_taper[None, :] * jnp.cos(phase_angle)
    sine_part = -hann_taper[None, :] * jnp.sin(phase_angle)
    return jnp.stack([cosine, sine_part], axis=1).reshape(2 * frequency_count, sample_count).astype(jnp.bfloat16)

def whiten(records, taper_table, overall_scale):
    spectra = jnp.einsum('ks,wcs->kwc', taper_table.astype(jnp.float32), records.astype(jnp.float32))
    mean_square = lax.optimization_barrier(jnp.mean(spectra * spectra, axis=0))
    factor = overall_scale / jnp.sqrt(mean_square + EPSILON)
    return (spectra * factor[None]).astype(jnp.bfloat16)

def make_rows(blocks):
    negated = jnp.stack([blocks[:, :, 1], -blocks[:, :, 0]], axis=2)
    joined = jnp.stack([blocks, negated], axis=-1)
    return joined.reshape(blocks.shape[:-1] + (2 * blocks.shape[-1],))

def pair_product(row_side, column_side):
    product = jnp.einsum('hgpwai,hgpwaj->ghaij', row_side, column_side)
    rounded = lax.optimization_barrier(product.astype(jnp.bfloat16))
    return rounded.astype(jnp.float32)

def reference(records):
    taper_table = dft_table(SAMPLES, FREQS, FIRST_BIN)
    block_count = CHANNELS // CH_DEV
    half_freq = FREQS // 2
    overall_scale = WINDOWS ** (-0.25)
    lower_mask = (jnp.arange(block_count) < HALF)[None, :, None, None]

    def accumulate(carry, group_records):
        near_sum, far_sum = carry
        whitened = whiten(group_records, taper_table, overall_scale)
        blocks = whitened.reshape(2, half_freq, 2, W_DEV, block_count, CH_DEV).astype(jnp.float32)
        row_side = make_rows(blocks)
        rounds = []
        for offset in range(HALF):
            rounds.append(pair_product(row_side, jnp.roll(blocks, -offset, axis=4)))
        near_part = jnp.stack(rounds, axis=2)
        low_part = pair_product(row_side, jnp.roll(blocks, -HALF, axis=4))[:, 0]
        high_part = pair_product(jnp.roll(row_side, -HALF, axis=4), blocks)[:, 1]
        far_part = jnp.where(lower_mask, low_part, high_part)
        return ((near_sum + near_part, far_sum + far_part), None)
    near_zero = jnp.zeros((half_freq, 2, HALF, block_count, 2 * CH_DEV, CH_DEV), jnp.float32)
    far_zero = jnp.zeros((half_freq, block_count, 2 * CH_DEV, CH_DEV), jnp.float32)
    grouped = records.reshape(N_TM, W_DEV, CHANNELS, SAMPLES)
    (near_sum, far_sum), unused = lax.scan(accumulate, (near_zero, far_zero), grouped)
    cross_near = near_sum.reshape(half_freq, 2, HALF, CHANNELS, 2, CH_DEV)
    cross_far = far_sum.reshape(half_freq, CHANNELS, 2, CH_DEV)
    return (cross_near, cross_far)
```

```python
import functools
import math

import jax
import jax.numpy as jnp
import ml_dtypes
import numpy as np
from jax import lax
from jax.experimental import pallas as pl
from jax.experimental.pallas import tpu as pltpu
from jax.sharding import PartitionSpec as P

FREQS = 64
FIRST_BIN = 32
EPSILON = 1e-06
VMEM_LIMIT = 48 * 1024 * 1024


def dft_table(sample_count, time_count):
    half_freq = FREQS // 2
    per_device = half_freq // time_count
    positions = np.arange(sample_count)
    taper = 0.5 - 0.5 * np.cos(2.0 * math.pi / sample_count * positions)
    bins = np.arange(FREQS) + FIRST_BIN
    angle = 2.0 * math.pi / sample_count * (bins[:, None] * positions[None, :] % sample_count)
    parts = np.stack([taper * np.cos(angle), -taper * np.sin(angle)], axis=0)
    ordered = parts.reshape(2, 2, time_count, per_device, sample_count).transpose(2, 3, 0, 1, 4)
    return ordered.reshape(2 * FREQS, sample_count).astype(ml_dtypes.bfloat16)


def whiten_kernel(scale, step_windows, window_count, table_ref, records_ref, out_ref, rows_ref):
    step = pl.program_id(0)
    bins = table_ref.shape[0]
    for local in range(step_windows):
        spectra = lax.dot_general(
            table_ref[...], records_ref[local], (((1,), (1,)), ((), ())), preferred_element_type=jnp.float32
        )
        mean_square = jnp.sum(spectra * spectra, axis=0, keepdims=True) * (1.0 / bins)
        whitened = spectra * (scale / jnp.sqrt(mean_square + EPSILON))
        window = step * step_windows + local
        for row in range(0, bins, 8):
            rows_ref[pl.ds(row * window_count + window, 8, stride=window_count), :] = whitened[row : row + 8]

    @pl.when(step == pl.num_programs(0) - 1)
    def _():
        rows = out_ref.shape[1]
        for target in range(out_ref.shape[0]):
            out_ref[target] = rows_ref[target * rows : (target + 1) * rows].astype(jnp.bfloat16)


def whiten(records, time_count):
    window_count, channels, samples = records.shape
    step_windows = 4 if window_count % 4 == 0 else 1
    bins = 2 * FREQS
    rows = bins * window_count // time_count
    scale = float(window_count * time_count) ** (-0.25)
    return pl.pallas_call(
        functools.partial(whiten_kernel, scale, step_windows, window_count),
        grid=(window_count // step_windows,),
        in_specs=[
            pl.BlockSpec((bins, samples), lambda i: (0, 0)),
            pl.BlockSpec((step_windows, channels, samples), lambda i: (i, 0, 0)),
        ],
        out_specs=pl.BlockSpec((time_count, rows, channels), lambda i: (0, 0, 0)),
        out_shape=jax.ShapeDtypeStruct((time_count, rows, channels), jnp.bfloat16),
        scratch_shapes=[pltpu.VMEM((bins * window_count, channels), jnp.float32)],
        compiler_params=pltpu.CompilerParams(vmem_limit_bytes=VMEM_LIMIT),
        name="whiten",
    )(jnp.asarray(dft_table(samples, time_count)), records)


def pair_kernel(window_count, lower_ref, masks_ref, *refs):
    near_out, far_out, near_sum, far_sum = refs[-4:]
    own_ref, far_ref = refs[0], refs[-5]
    near_refs = refs[1:-5]
    groups = own_ref.shape[0]
    width = own_ref.shape[2]
    lower = lower_ref[0] > 0
    half = jnp.where(lower, 0, 1)

    def rotated(block):
        middle = block.shape[0] // 2
        return jnp.concatenate([block[middle:], block[:middle]], axis=0)

    def product(left, right):
        value = lax.dot_general(left, right, (((0,), (0,)), ((), ())), preferred_element_type=jnp.float32)
        return value.astype(jnp.bfloat16).astype(jnp.float32)

    near_total = None
    far_total = None
    for group in range(groups):
        own = own_ref[group]
        turned = rotated(own)
        left = jnp.concatenate(
            [own * masks_ref[0], turned * masks_ref[1], own * masks_ref[2], turned * masks_ref[3]], axis=1
        )
        right = jnp.concatenate([own] + [ref[group] for ref in near_refs], axis=1)
        near = product(left, right)
        far = far_ref[group]
        first = jnp.where(lower, own, far)
        second = jnp.where(lower, far, own)
        far_left = jnp.concatenate(
            [first * masks_ref[2 * half], rotated(first) * masks_ref[2 * half + 1]], axis=1
        )
        far = product(far_left, second)
        if group == 0:
            near_sum[...] = near
            far_sum[...] = far
        else:
            near_sum[...] += near
            far_sum[...] += far
    for h in range(2):
        for r in range(1 + len(near_refs)):
            for p in range(2):
                start = (2 * h + p) * width
                near_out[0, h, r, pl.ds(p, width, stride=2), :] = near_sum[
                    start : start + width, r * width : (r + 1) * width
                ]
    for p in range(2):
        far_out[0, pl.ds(p, width, stride=2), :] = far_sum[p * width : (p + 1) * width, :]


def pair_stack(own, near_mates, far_mate, window_count):
    groups, all_rows, width = own.shape
    rows = 4 * window_count
    per_device = all_rows // rows
    rounds = 1 + len(near_mates)
    lower = (lax.axis_index("chan") < lax.axis_size("chan") // 2).astype(jnp.int32).reshape(1)
    index = np.arange(rows)
    part, half = index // (2 * window_count), index // window_count % 2
    sign = np.where(part == 0, 1.0, -1.0)
    masks = np.stack([half == 0, (half == 0) * sign, half == 1, (half == 1) * sign])
    masks = np.broadcast_to(masks[:, :, None], (4, rows, width)).astype(ml_dtypes.bfloat16)
    block = pl.BlockSpec((groups, rows, width), lambda g, *_: (0, g, 0))
    return pl.pallas_call(
        functools.partial(pair_kernel, window_count),
        grid_spec=pltpu.PrefetchScalarGridSpec(
            num_scalar_prefetch=1,
            grid=(per_device,),
            in_specs=[pl.BlockSpec((4, rows, width), lambda g, *_: (0, 0, 0))] + [block] * (rounds + 1),
            out_specs=[
                pl.BlockSpec((1, 2, rounds, 2 * width, width), lambda g, *_: (g, 0, 0, 0, 0)),
                pl.BlockSpec((1, 2 * width, width), lambda g, *_: (g, 0, 0)),
            ],
            scratch_shapes=[
                pltpu.VMEM((4 * width, rounds * width), jnp.float32),
                pltpu.VMEM((2 * width, width), jnp.float32),
            ],
        ),
        out_shape=[
            jax.ShapeDtypeStruct((per_device, 2, rounds, 2 * width, width), jnp.float32),
            jax.ShapeDtypeStruct((per_device, 2 * width, width), jnp.float32),
        ],
        compiler_params=pltpu.CompilerParams(vmem_limit_bytes=VMEM_LIMIT),
        name="pair_stack",
    )(lower, jnp.asarray(masks), own, *near_mates, far_mate)


def shifted(value, steps):
    count = lax.axis_size("chan")
    return lax.ppermute(value, "chan", [(source, (source + steps) % count) for source in range(count)])


def body(records):
    window_count, width = records.shape[:2]
    time_count, chan_count = lax.axis_size("tm"), lax.axis_size("chan")
    whitened = whiten(records, time_count)
    own = lax.all_to_all(whitened, "tm", split_axis=0, concat_axis=0, tiled=True)
    mates = [shifted(own, -offset) for offset in range(1, chan_count // 2 + 1)]
    near, far = pair_stack(own, mates[:-1], mates[-1], window_count)
    near = near.reshape(near.shape[:3] + (width, 2, width))
    return near, far.reshape(far.shape[0], width, 2, width)


def solution(mesh):
    return jax.shard_map(
        body,
        mesh=mesh,
        in_specs=(P("tm", "chan", None),),
        out_specs=(P("tm", None, None, "chan", None, None), P("tm", "chan", None, None)),
        check_vma=False,
    )
```

```python
import functools
import math

import jax
import jax.numpy as jnp
import ml_dtypes
import numpy as np
from jax import lax
from jax.experimental import pallas as pl
from jax.experimental.pallas import tpu as pltpu
from jax.sharding import PartitionSpec as P

FREQS = 64
FIRST_BIN = 32
EPSILON = 1e-06
VMEM_LIMIT = 48 * 1024 * 1024


def dft_table(sample_count, time_count):
    half_freq = FREQS // 2
    per_device = half_freq // time_count
    positions = np.arange(sample_count)
    taper = 0.5 - 0.5 * np.cos(2.0 * math.pi / sample_count * positions)
    bins = np.arange(FREQS) + FIRST_BIN
    angle = 2.0 * math.pi / sample_count * (bins[:, None] * positions[None, :] % sample_count)
    parts = np.stack([taper * np.cos(angle), -taper * np.sin(angle)], axis=0)
    ordered = parts.reshape(2, 2, time_count, per_device, sample_count).transpose(2, 3, 0, 1, 4)
    return ordered.reshape(2 * FREQS, sample_count).astype(ml_dtypes.bfloat16)


def whiten_kernel(scale, step_windows, counts, target_of, table_hbm, records_hbm, *refs):
    out_refs = refs[: len(counts)]
    table_ref, records_ref, rows_ref, table_sem, record_sems = refs[len(counts) :]
    window_count, channels, samples = records_ref.shape
    bins = table_ref.shape[1]
    table_copy = pltpu.make_async_copy(table_hbm, table_ref, table_sem)
    table_copy.start()
    copies = []
    for step in range(window_count // step_windows):
        span = pl.ds(step * step_windows, step_windows)
        copies.append(pltpu.make_async_copy(records_hbm.at[span], records_ref.at[span], record_sems.at[step]))
        copies[-1].start()
    table_copy.wait()
    for step, copy in enumerate(copies):
        copy.wait()
        windows = records_ref[step * step_windows : (step + 1) * step_windows]
        spectra = jnp.dot(
            windows.reshape(step_windows * channels, samples), table_ref[...], preferred_element_type=jnp.float32
        )
        for local in range(step_windows):
            block = spectra[local * channels : (local + 1) * channels].T
            mean_square = jnp.sum(block * block, axis=0, keepdims=True) * (1.0 / bins)
            whitened = block * (scale / jnp.sqrt(mean_square + EPSILON))
            window = step * step_windows + local
            for row in range(0, bins, 8):
                rows_ref[pl.ds(row * window_count + window, 8, stride=window_count), :] = whitened[row : row + 8]
    place = 0
    for out_ref, count in zip(out_refs, counts):
        rows = out_ref.shape[1]
        for index in range(count):
            start = pl.multiple_of(target_of(place) * rows, 16)
            out_ref[index] = rows_ref[pl.ds(start, rows), :].astype(jnp.bfloat16)
            place += 1


def whiten(records, time_count, target_of, counts, sizes):
    window_count, channels, samples = records.shape
    step_windows = 4 if window_count % 4 == 0 else 1
    bins = 2 * FREQS
    rows = bins * window_count // time_count
    scale = float(window_count * time_count) ** (-0.25)
    return pl.pallas_call(
        functools.partial(whiten_kernel, scale, step_windows, counts, target_of),
        in_specs=[pl.BlockSpec(memory_space=pltpu.HBM)] * 2,
        out_specs=[pl.BlockSpec(memory_space=pltpu.VMEM)] * len(sizes),
        out_shape=[jax.ShapeDtypeStruct((size, rows, channels), jnp.bfloat16) for size in sizes],
        scratch_shapes=[
            pltpu.VMEM((samples, bins), jnp.bfloat16),
            pltpu.VMEM(records.shape, jnp.bfloat16),
            pltpu.VMEM((bins * window_count, channels), jnp.float32),
            pltpu.SemaphoreType.DMA,
            pltpu.SemaphoreType.DMA((window_count // step_windows,)),
        ],
        compiler_params=pltpu.CompilerParams(vmem_limit_bytes=VMEM_LIMIT),
        name="whiten",
    )(jnp.asarray(dft_table(samples, time_count).T.copy()), records)


def pair_kernel(chunk_count, operand_count, lower_ref, masks_ref, *refs):
    near_out, far_out, near_sum, far_sum = refs[-4:]
    near_before, far_before = refs[operand_count:-4] or (None, None)
    arrays = [refs[start : start + chunk_count] for start in range(0, operand_count, chunk_count)]
    own_refs, near_refs, far_refs = arrays[0], arrays[1:-1], arrays[-1]
    width = own_refs[0].shape[2]
    lower = lower_ref[0] > 0
    half = jnp.where(lower, 0, 1)

    def rotated(block):
        middle = block.shape[0] // 2
        return jnp.concatenate([block[middle:], block[:middle]], axis=0)

    def product(left, right):
        value = lax.dot_general(left, right, (((0,), (0,)), ((), ())), preferred_element_type=jnp.float32)
        return value.astype(jnp.bfloat16).astype(jnp.float32)

    first_group = True
    for chunk in range(chunk_count):
        for group in range(own_refs[chunk].shape[0]):
            own = own_refs[chunk][group]
            turned = rotated(own)
            left = jnp.concatenate(
                [own * masks_ref[0], turned * masks_ref[1], own * masks_ref[2], turned * masks_ref[3]], axis=1
            )
            right = jnp.concatenate([own] + [near[chunk][group] for near in near_refs], axis=1)
            near = product(left, right)
            far = far_refs[chunk][group]
            first = jnp.where(lower, own, far)
            second = jnp.where(lower, far, own)
            far_left = jnp.concatenate(
                [first * masks_ref[2 * half], rotated(first) * masks_ref[2 * half + 1]], axis=1
            )
            far = product(far_left, second)
            if first_group:
                near_sum[...] = near
                far_sum[...] = far
            else:
                near_sum[...] += near
                far_sum[...] += far
            first_group = False
    for h in range(2):
        for r in range(1 + len(near_refs)):
            for p in range(2):
                start = (2 * h + p) * width
                place = (0, h, r, pl.ds(p, width, stride=2), slice(None))
                total = near_sum[start : start + width, r * width : (r + 1) * width]
                near_out[place] = total if near_before is None else total + near_before[place]
    for p in range(2):
        place = (0, pl.ds(p, width, stride=2), slice(None))
        total = far_sum[p * width : (p + 1) * width, :]
        far_out[place] = total if far_before is None else total + far_before[place]


def pair_stack(own, near, far, window_count, before=()):
    all_rows, width = own[0].shape[1:]
    rows = 4 * window_count
    per_device = all_rows // rows
    rounds = 1 + len(near)
    lower = (lax.axis_index("chan") < lax.axis_size("chan") // 2).astype(jnp.int32).reshape(1)
    index = np.arange(rows)
    part, half = index // (2 * window_count), index // window_count % 2
    sign = np.where(part == 0, 1.0, -1.0)
    masks = np.stack([half == 0, (half == 0) * sign, half == 1, (half == 1) * sign])
    masks = np.broadcast_to(masks[:, :, None], (4, rows, width)).astype(ml_dtypes.bfloat16)
    operands = [chunk for chunks in [own] + near + [far] for chunk in chunks]
    sums = [
        pl.BlockSpec((1, 2, rounds, 2 * width, width), lambda g, *_: (g, 0, 0, 0, 0)),
        pl.BlockSpec((1, 2 * width, width), lambda g, *_: (g, 0, 0)),
    ]
    return pl.pallas_call(
        functools.partial(pair_kernel, len(own), len(operands)),
        grid_spec=pltpu.PrefetchScalarGridSpec(
            num_scalar_prefetch=1,
            grid=(per_device,),
            in_specs=[pl.BlockSpec((4, rows, width), lambda g, *_: (0, 0, 0))]
            + [pl.BlockSpec((chunk.shape[0], rows, width), lambda g, *_: (0, g, 0)) for chunk in operands]
            + (sums if before else []),
            out_specs=sums,
            scratch_shapes=[
                pltpu.VMEM((4 * width, rounds * width), jnp.float32),
                pltpu.VMEM((2 * width, width), jnp.float32),
            ],
        ),
        out_shape=[
            jax.ShapeDtypeStruct((per_device, 2, rounds, 2 * width, width), jnp.float32),
            jax.ShapeDtypeStruct((per_device, 2 * width, width), jnp.float32),
        ],
        input_output_aliases={2 + len(operands) + i: i for i in range(len(before))},
        compiler_params=pltpu.CompilerParams(vmem_limit_bytes=VMEM_LIMIT),
        name="pair_stack",
    )(lower, jnp.asarray(masks), *operands, *before)


def shifted(value, steps):
    count = lax.axis_size("chan")
    return lax.ppermute(value, "chan", [(source, (source + steps) % count) for source in range(count)])


def swapped(value, axis, bit):
    return lax.ppermute(value, axis, [(source, source ^ bit) for source in range(lax.axis_size(axis))])


def moved(value, steps):
    count = lax.axis_size("tm")
    return lax.ppermute(value, "tm", [(source, (source + 2 * steps) % count) for source in range(count)])


def phase_kernel(kept, copies, *refs):
    semaphores = refs[-1]
    outs = refs[kept:-1]
    odd = lax.rem(lax.axis_index("chan"), 2) == 1

    def run(chosen):
        started = []
        for place, (when, source, source_index, target, target_index) in enumerate(copies):
            if when == chosen:
                from_ref = outs[source] if source_index is None else outs[source].at[source_index]
                to_ref = outs[target] if target_index is None else outs[target].at[target_index]
                started.append(pltpu.make_async_copy(from_ref, to_ref, semaphores.at[place]))
                started[-1].start()
        for copy in started:
            copy.wait()

    run("always")
    if any(copy[0] != "always" for copy in copies):
        pl.when(odd)(functools.partial(run, "odd"))
        pl.when(jnp.logical_not(odd))(functools.partial(run, "even"))


def phase(operands, copies, like=()):
    shapes = [jax.ShapeDtypeStruct(x.shape, x.dtype) for x in list(operands) + [operands[i] for i in like]]
    anywhere = pl.BlockSpec(memory_space=pl.ANY)
    return pl.pallas_call(
        functools.partial(phase_kernel, len(operands), copies),
        in_specs=[anywhere] * len(operands),
        out_specs=[anywhere] * len(shapes),
        out_shape=shapes,
        input_output_aliases={i: i for i in range(len(operands))},
        scratch_shapes=[pltpu.SemaphoreType.DMA((max(1, len(copies)),))],
        compiler_params=pltpu.CompilerParams(vmem_limit_bytes=VMEM_LIMIT),
        cost_estimate=pl.CostEstimate(flops=0, bytes_accessed=0, transcendentals=0),
        name="phase",
    )(*operands)


def choose(own, far, target):
    return [("odd", own, None, target, None), ("even", far, None, target, None)]


def square_stack(records):
    window_count = records.shape[0]
    count = lax.axis_size("tm")

    def target_of(place):
        me = lax.axis_index("tm")
        core = me % 2 if place < 4 else 1 - me % 2
        return (me // 2 + (2, 0, 1, 3)[place % 4]) % (count // 2) * 2 + core

    opposite, here, after, before, other_core = whiten(records, count, target_of, (1, 1, 1, 1, 4), (1, 2, 2, 2, 4))
    far_swap = functools.partial(swapped, axis="chan", bit=2)
    near_swap = functools.partial(swapped, axis="chan", bit=1)
    stack = functools.partial(pair_stack, window_count=window_count)

    core = swapped(other_core, "tm", 1)
    last = core[:1]
    here, after, before, core = phase(
        [here, after, before, core],
        [("always", 3, 1, 0, 1), ("always", 3, 2, 1, 1), ("always", 3, 3, 2, 1)],
    )
    after = moved(after, 1)
    here_far = far_swap(here)

    here, here_far, after, before, here_send = phase([here, here_far, after, before], choose(0, 1, 4), like=(0,))
    before = moved(before, 3)
    after_far = far_swap(after)
    here_near = near_swap(here_send)

    after, after_far, before, opposite, here_near, after_send = phase(
        [after, after_far, before, opposite, here_near], choose(0, 1, 5), like=(0,)
    )
    two = moved(opposite, 2)
    before_far = far_swap(before)
    after_near = near_swap(after_send)
    near_sum, far_sum = stack([here], [[here_near]], [here_far])

    before, before_far, two, last, after_near, far_sum, before_send = phase(
        [before, before_far, two, last, after_near, far_sum], choose(0, 1, 6), like=(0,)
    )
    last = moved(last, 2)
    two_far = far_swap(two)
    before_near = near_swap(before_send)
    near_sum, far_sum = stack([after], [[after_near]], [after_far], before=(near_sum, far_sum))

    two, two_far, last, before_near, far_sum, two_send = phase(
        [two, two_far, last, before_near, far_sum], choose(0, 1, 5), like=(0,)
    )
    last_far = far_swap(last)
    last_near = shifted(last, -1)
    two_near = near_swap(two_send)
    near_sum, far_sum = stack([before], [[before_near]], [before_far], before=(near_sum, far_sum))
    return stack([two, last], [[two_near, last_near]], [two_far, last_far], before=(near_sum, far_sum))


def plain_stack(records):
    count, chan_count = lax.axis_size("tm"), lax.axis_size("chan")
    whitened = whiten(records, count, lambda place: place, (count,), (count,))[0]
    own = lax.all_to_all(whitened, "tm", split_axis=0, concat_axis=0, tiled=True)
    mates = [shifted(own, -offset) for offset in range(1, chan_count // 2 + 1)]
    return pair_stack([own], [[mate] for mate in mates[:-1]], [mates[-1]], records.shape[0])


def body(records):
    width = records.shape[1]
    square = lax.axis_size("tm") == 8 and lax.axis_size("chan") == 4
    near, far = (square_stack if square else plain_stack)(records)
    near = near.reshape(near.shape[:3] + (width, 2, width))
    return near, far.reshape(far.shape[0], width, 2, width)


def solution(mesh):
    return jax.shard_map(
        body,
        mesh=mesh,
        in_specs=(P("tm", "chan", None),),
        out_specs=(P("tm", None, None, "chan", None, None), P("tm", "chan", None, None)),
        check_vma=False,
    )
```

```python
import functools
import math

import jax
import jax.numpy as jnp
import ml_dtypes
import numpy as np
from jax import lax
from jax.experimental import pallas as pl
from jax.experimental.pallas import tpu as pltpu
from jax.sharding import PartitionSpec as P

FREQS = 64
FIRST_BIN = 32
EPSILON = 1e-06
WHITEN_VMEM = 52 * 1024 * 1024
VMEM_LIMIT = 16 * 1024 * 1024


def dft_table(bins, samples):
    row = lax.broadcasted_iota(jnp.int32, (bins, samples), 0)
    position = lax.broadcasted_iota(jnp.int32, (bins, samples), 1)
    frequency = FIRST_BIN + FREQS // 2 * (row % 2) + row // 4
    phase_index = (frequency * position + samples // 4 * (row // 2 % 2)) % samples
    scale = 2.0 * math.pi / samples
    taper = 0.5 - 0.5 * jnp.cos(scale * lax.broadcasted_iota(jnp.int32, (1, samples), 1).astype(jnp.float32))
    return (taper * jnp.cos(scale * phase_index.astype(jnp.float32))).astype(jnp.bfloat16)


def whiten_kernel(scale, step_windows, counts, target_of, records_hbm, *refs):
    out_refs = refs[: len(counts)]
    table_ref, records_ref, rows_ref, record_sems = refs[len(counts) :]
    window_count, channels, samples = records_ref.shape
    bins = table_ref.shape[0]
    steps = window_count // step_windows

    def record_copy(step):
        span = pl.ds(step * step_windows, step_windows)
        return pltpu.make_async_copy(records_hbm.at[span], records_ref.at[span], record_sems.at[step])

    for step in range(min(2, steps)):
        record_copy(step).start()
    table_ref[...] = dft_table(bins, samples)
    for step in range(steps):
        record_copy(step).wait()
        if step + 2 < steps:
            record_copy(step + 2).start()
        windows = records_ref[step * step_windows : (step + 1) * step_windows]
        spectra = lax.dot_general(
            table_ref[...],
            windows.reshape(step_windows * channels, samples),
            (((1,), (1,)), ((), ())),
            preferred_element_type=jnp.float32,
        )
        mean_square = jnp.sum(spectra * spectra, axis=0, keepdims=True) * (1.0 / bins)
        whitened = spectra * (scale / jnp.sqrt(mean_square + EPSILON))
        for local in range(step_windows):
            window = step * step_windows + local
            for row in range(0, bins, 8):
                rows_ref[pl.ds(row * window_count + window, 8, stride=window_count), :] = whitened[
                    row : row + 8, local * channels : (local + 1) * channels
                ]
    place = 0
    for out_ref, count in zip(out_refs, counts):
        rows = out_ref.shape[1]
        for index in range(count):
            start = pl.multiple_of(target_of(place) * rows, 16)
            out_ref[index] = rows_ref[pl.ds(start, rows), :].astype(jnp.bfloat16)
            place += 1


def whiten(records, time_count, target_of, counts, sizes):
    window_count, channels, samples = records.shape
    step_windows = window_count // 4 if window_count % 4 == 0 else window_count
    bins = 2 * FREQS
    rows = bins * window_count // time_count
    scale = float(window_count * time_count) ** (-0.25)
    return pl.pallas_call(
        functools.partial(whiten_kernel, scale, step_windows, counts, target_of),
        in_specs=[pl.BlockSpec(memory_space=pltpu.HBM)],
        out_specs=[pl.BlockSpec(memory_space=pltpu.VMEM)] * len(sizes),
        out_shape=[jax.ShapeDtypeStruct((size, rows, channels), jnp.bfloat16) for size in sizes],
        scratch_shapes=[
            pltpu.VMEM((bins, samples), jnp.bfloat16),
            pltpu.VMEM(records.shape, jnp.bfloat16),
            pltpu.VMEM((bins * window_count, channels), jnp.float32),
            pltpu.SemaphoreType.DMA((window_count // step_windows,)),
        ],
        compiler_params=pltpu.CompilerParams(vmem_limit_bytes=WHITEN_VMEM),
        name="whiten",
    )(records)


def pair_kernel(chunk_count, operand_count, lower_ref, masks_ref, *refs):
    near_out, far_out, near_sum, far_sum = refs[-4:]
    near_before, far_before = refs[operand_count:-4] or (None, None)
    arrays = [refs[start : start + chunk_count] for start in range(0, operand_count, chunk_count)]
    own_refs, near_refs, far_refs = arrays[0], arrays[1:-1], arrays[-1]
    width = own_refs[0].shape[2]
    lower = lower_ref[0] > 0
    half = jnp.where(lower, 0, 1)

    def rotated(block):
        middle = block.shape[0] // 2
        return jnp.concatenate([block[middle:], block[:middle]], axis=0)

    def product(left, right):
        value = lax.dot_general(left, right, (((0,), (0,)), ((), ())), preferred_element_type=jnp.float32)
        return value.astype(jnp.bfloat16).astype(jnp.float32)

    first_group = True
    for chunk in range(chunk_count):
        for group in range(own_refs[chunk].shape[0]):
            own = own_refs[chunk][group]
            turned = rotated(own)
            left = jnp.concatenate(
                [own * masks_ref[0], turned * masks_ref[1], own * masks_ref[2], turned * masks_ref[3]], axis=1
            )
            right = jnp.concatenate([own] + [near[chunk][group] for near in near_refs], axis=1)
            near = product(left, right)
            far = far_refs[chunk][group]
            first = jnp.where(lower, own, far)
            second = jnp.where(lower, far, own)
            far_left = jnp.concatenate(
                [first * masks_ref[2 * half], rotated(first) * masks_ref[2 * half + 1]], axis=1
            )
            far = product(far_left, second)
            if first_group:
                near_sum[...] = near
                far_sum[...] = far
            else:
                near_sum[...] += near
                far_sum[...] += far
            first_group = False
    for h in range(2):
        for r in range(1 + len(near_refs)):
            for p in range(2):
                start = (2 * h + p) * width
                place = (0, h, r, pl.ds(p, width, stride=2), slice(None))
                total = near_sum[start : start + width, r * width : (r + 1) * width]
                near_out[place] = total if near_before is None else total + near_before[place]
    for p in range(2):
        place = (0, pl.ds(p, width, stride=2), slice(None))
        total = far_sum[p * width : (p + 1) * width, :]
        far_out[place] = total if far_before is None else total + far_before[place]


def pair_stack(own, near, far, window_count, before=(), in_place=False):
    all_rows, width = own[0].shape[1:]
    rows = 4 * window_count
    per_device = all_rows // rows
    rounds = 1 + len(near)
    lower = (lax.axis_index("chan") < lax.axis_size("chan") // 2).astype(jnp.int32).reshape(1)
    index = np.arange(rows)
    part, half = index // (2 * window_count), index // window_count % 2
    sign = np.where(part == 0, 1.0, -1.0)
    masks = np.stack([half == 0, (half == 0) * sign, half == 1, (half == 1) * sign])
    masks = np.broadcast_to(masks[:, :, None], (4, rows, width)).astype(ml_dtypes.bfloat16)
    operands = [chunk for chunks in [own] + near + [far] for chunk in chunks]
    sums = [
        pl.BlockSpec((1, 2, rounds, 2 * width, width), lambda g, *_: (g, 0, 0, 0, 0)),
        pl.BlockSpec((1, 2 * width, width), lambda g, *_: (g, 0, 0)),
    ]
    return pl.pallas_call(
        functools.partial(pair_kernel, len(own), len(operands)),
        grid_spec=pltpu.PrefetchScalarGridSpec(
            num_scalar_prefetch=1,
            grid=(per_device,),
            in_specs=[pl.BlockSpec((4, rows, width), lambda g, *_: (0, 0, 0))]
            + [pl.BlockSpec((chunk.shape[0], rows, width), lambda g, *_: (0, g, 0)) for chunk in operands]
            + (sums if before else []),
            out_specs=sums,
            scratch_shapes=[
                pltpu.VMEM((4 * width, rounds * width), jnp.float32),
                pltpu.VMEM((2 * width, width), jnp.float32),
            ],
        ),
        out_shape=[
            jax.ShapeDtypeStruct((per_device, 2, rounds, 2 * width, width), jnp.float32),
            jax.ShapeDtypeStruct((per_device, 2 * width, width), jnp.float32),
        ],
        input_output_aliases={2 + len(operands) + i: i for i in range(len(before) if in_place else 0)},
        compiler_params=pltpu.CompilerParams(vmem_limit_bytes=VMEM_LIMIT),
        name="pair_stack",
    )(lower, jnp.asarray(masks), *operands, *before)


def shifted(value, steps):
    count = lax.axis_size("chan")
    return lax.ppermute(value, "chan", [(source, (source + steps) % count) for source in range(count)])


def swapped(value, axis, bit):
    return lax.ppermute(value, axis, [(source, source ^ bit) for source in range(lax.axis_size(axis))])


def moved(value, steps):
    count = lax.axis_size("tm")
    return lax.ppermute(value, "tm", [(source, (source + 2 * steps) % count) for source in range(count)])


def phase_kernel(kept, made, copies, *refs):
    sources, outs = refs[kept : len(refs) - kept - made], refs[len(refs) - made :]
    odd = lax.rem(lax.axis_index("chan"), 2) == 1

    def run(chosen):
        for when, source, target, first in copies:
            if when == chosen:
                outs[target][first : first + sources[source].shape[0]] = sources[source][...]

    run("always")
    if any(copy[0] != "always" for copy in copies):
        pl.when(odd)(functools.partial(run, "odd"))
        pl.when(jnp.logical_not(odd))(functools.partial(run, "even"))


def phase(kept, sources=(), counts=(), copies=()):
    made = [jax.ShapeDtypeStruct((count,) + sources[0].shape[1:], sources[0].dtype) for count in counts]
    anywhere, vmem = pl.BlockSpec(memory_space=pl.ANY), pl.BlockSpec(memory_space=pltpu.VMEM)
    return pl.pallas_call(
        functools.partial(phase_kernel, len(kept), len(made), tuple(copies)),
        in_specs=[anywhere] * len(kept) + [vmem] * len(sources),
        out_specs=[anywhere] * len(kept) + [vmem] * len(made),
        out_shape=[jax.ShapeDtypeStruct(x.shape, x.dtype) for x in kept] + made,
        input_output_aliases={i: i for i in range(len(kept))},
        compiler_params=pltpu.CompilerParams(vmem_limit_bytes=VMEM_LIMIT),
        name="phase",
    )(*kept, *sources)


def near_payload(kept, own, far):
    return phase(kept, [own, far], [own.shape[0]], [("odd", 0, 0, 0), ("even", 1, 0, 0)])


def square_stack(records):
    window_count = records.shape[0]
    count = lax.axis_size("tm")

    def target_of(place):
        me = lax.axis_index("tm")
        core = me % 2 if place < 4 else 1 - me % 2
        return (me // 2 + (1, 2, 3, 0)[place % 4]) % (count // 2) * 2 + core

    after_one, opposite, before, here, core = whiten(records, count, target_of, (1, 1, 1, 1, 4), (1, 1, 1, 1, 4))
    far_swap = functools.partial(swapped, axis="chan", bit=2)
    near_swap = functools.partial(swapped, axis="chan", bit=1)
    stack = functools.partial(pair_stack, window_count=window_count)
    grow = functools.partial(stack, in_place=True)
    token = jnp.zeros((8, 128), jnp.float32)

    after_one = moved(after_one, 1)
    core = swapped(core, "tm", 1)
    core_after, core_last, core_before, core_here = (core[i : i + 1] for i in range(4))
    token, here, after_two, last, before_two = phase(
        [token],
        [here, core_here, core_after, core_last, core_before],
        [2, 1, 1, 1],
        [("always", 0, 0, 0), ("always", 1, 0, 1), ("always", 2, 1, 0), ("always", 3, 2, 0), ("always", 4, 3, 0)],
    )
    after_two = moved(after_two, 1)
    here_far = far_swap(here)

    token, after_one, before = phase([token, after_one, before])
    before_one = moved(before, 3)

    token, before_two, after = phase([token, before_two], [after_one, after_two], [2], [("always", 0, 0, 0), ("always", 1, 0, 1)])
    before_two = moved(before_two, 3)
    after_far = far_swap(after)

    token, here_send = near_payload([token], here, here_far)
    here_near = near_swap(here_send)

    token, before_one, opposite = phase([token, before_one, opposite])
    two = moved(opposite, 2)

    token, last, before = phase([token, last], [before_one, before_two], [2], [("always", 0, 0, 0), ("always", 1, 0, 1)])
    last = moved(last, 2)
    before_far = far_swap(before)

    token, after_send = near_payload([token], after, after_far)
    after_near = near_swap(after_send)
    near_sum, far_sum = stack([here], [[here_near]], [here_far])

    token, far_sum, before_send = near_payload([token, far_sum], before, before_far)
    before_near = near_swap(before_send)

    token, two = phase([token, two])
    two_far = far_swap(two)
    near_sum, far_sum = grow([after], [[after_near]], [after_far], before=(near_sum, far_sum))

    token, far_sum, two_send = near_payload([token, far_sum], two, two_far)
    two_near = near_swap(two_send)

    last_near = shifted(last, -1)
    last_far = far_swap(last)
    near_sum, far_sum = grow([before], [[before_near]], [before_far], before=(near_sum, far_sum))
    return stack([two, last], [[two_near, last_near]], [two_far, last_far], before=(near_sum, far_sum))


def plain_stack(records):
    count, chan_count = lax.axis_size("tm"), lax.axis_size("chan")
    whitened = whiten(records, count, lambda place: place, (count,), (count,))[0]
    own = lax.all_to_all(whitened, "tm", split_axis=0, concat_axis=0, tiled=True)
    mates = [shifted(own, -offset) for offset in range(1, chan_count // 2 + 1)]
    return pair_stack([own], [[mate] for mate in mates[:-1]], [mates[-1]], records.shape[0])


def body(records):
    width = records.shape[1]
    square = lax.axis_size("tm") == 8 and lax.axis_size("chan") == 4
    near, far = (square_stack if square else plain_stack)(records)
    near = near.reshape(near.shape[:3] + (width, 2, width))
    return near, far.reshape(far.shape[0], width, 2, width)


def solution(mesh):
    return jax.shard_map(
        body,
        mesh=mesh,
        in_specs=(P("tm", "chan", None),),
        out_specs=(P("tm", None, None, "chan", None, None), P("tm", "chan", None, None)),
        check_vma=False,
    )
```

```python
import functools
import math

import jax
import jax.numpy as jnp
import ml_dtypes
import numpy as np
from jax import lax
from jax.experimental import pallas as pl
from jax.experimental.pallas import tpu as pltpu
from jax.sharding import PartitionSpec as P

FREQS = 64
FIRST_BIN = 32
EPSILON = 1e-06
WHITEN_VMEM = 52 * 1024 * 1024
VMEM_LIMIT = 16 * 1024 * 1024


def dft_table(bins, samples):
    row = lax.broadcasted_iota(jnp.int32, (bins, samples), 0)
    position = lax.broadcasted_iota(jnp.int32, (bins, samples), 1)
    frequency = FIRST_BIN + FREQS // 2 * (row % 2) + row // 4
    phase_index = (frequency * position + samples // 4 * (row // 2 % 2)) % samples
    scale = 2.0 * math.pi / samples
    taper = 0.5 - 0.5 * jnp.cos(scale * lax.broadcasted_iota(jnp.int32, (1, samples), 1).astype(jnp.float32))
    return (taper * jnp.cos(scale * phase_index.astype(jnp.float32))).astype(jnp.bfloat16)


def whiten_kernel(scale, step_windows, counts, target_of, records_hbm, *refs):
    out_refs = refs[: len(counts)]
    table_ref, records_ref, rows_ref, record_sems = refs[len(counts) :]
    window_count, channels, samples = records_ref.shape
    bins = table_ref.shape[0]
    steps = window_count // step_windows

    def record_copy(step):
        span = pl.ds(step * step_windows, step_windows)
        return pltpu.make_async_copy(records_hbm.at[span], records_ref.at[span], record_sems.at[step])

    for step in range(min(2, steps)):
        record_copy(step).start()
    table_ref[...] = dft_table(bins, samples)
    for step in range(steps):
        record_copy(step).wait()
        if step + 2 < steps:
            record_copy(step + 2).start()
        windows = records_ref[step * step_windows : (step + 1) * step_windows]
        spectra = lax.dot_general(
            table_ref[...],
            windows.reshape(step_windows * channels, samples),
            (((1,), (1,)), ((), ())),
            preferred_element_type=jnp.float32,
        )
        mean_square = jnp.sum(spectra * spectra, axis=0, keepdims=True) * (1.0 / bins)
        whitened = spectra * (scale / jnp.sqrt(mean_square + EPSILON))
        for local in range(step_windows):
            window = step * step_windows + local
            for row in range(0, bins, 8):
                rows_ref[pl.ds(row * window_count + window, 8, stride=window_count), :] = whitened[
                    row : row + 8, local * channels : (local + 1) * channels
                ]
    place = 0
    for out_ref, count in zip(out_refs, counts):
        rows = out_ref.shape[1]
        for index in range(count):
            start = pl.multiple_of(target_of(place) * rows, 16)
            out_ref[index] = rows_ref[pl.ds(start, rows), :].astype(jnp.bfloat16)
            place += 1


def whiten(records, time_count, target_of, counts, sizes):
    window_count, channels, samples = records.shape
    step_windows = window_count // 4 if window_count % 4 == 0 else window_count
    bins = 2 * FREQS
    rows = bins * window_count // time_count
    scale = float(window_count * time_count) ** (-0.25)
    return pl.pallas_call(
        functools.partial(whiten_kernel, scale, step_windows, counts, target_of),
        in_specs=[pl.BlockSpec(memory_space=pltpu.HBM)],
        out_specs=[pl.BlockSpec(memory_space=pltpu.VMEM)] * len(sizes),
        out_shape=[jax.ShapeDtypeStruct((size, rows, channels), jnp.bfloat16) for size in sizes],
        scratch_shapes=[
            pltpu.VMEM((bins, samples), jnp.bfloat16),
            pltpu.VMEM(records.shape, jnp.bfloat16),
            pltpu.VMEM((bins * window_count, channels), jnp.float32),
            pltpu.SemaphoreType.DMA((window_count // step_windows,)),
        ],
        compiler_params=pltpu.CompilerParams(vmem_limit_bytes=WHITEN_VMEM),
        name="whiten",
    )(records)


def pair_kernel(chunk_count, operand_count, streamed, lower_ref, masks_ref, *refs):
    if streamed:
        near_hbm, far_hbm, near_sum, far_sum, near_out, far_out, sems = refs[-7:]
        near_before, far_before = refs[operand_count:-7] or (None, None)
        slot = pl.program_id(0)
    else:
        near_out, far_out, near_sum, far_sum = refs[-4:]
        near_before, far_before = refs[operand_count:-4] or (None, None)
        slot = 0
    arrays = [refs[start : start + chunk_count] for start in range(0, operand_count, chunk_count)]
    own_refs, near_refs, far_refs = arrays[0], arrays[1:-1], arrays[-1]
    width = own_refs[0].shape[2]
    lower = lower_ref[0] > 0
    half = jnp.where(lower, 0, 1)

    def rotated(block):
        middle = block.shape[0] // 2
        return jnp.concatenate([block[middle:], block[:middle]], axis=0)

    def product(left, right):
        value = lax.dot_general(left, right, (((0,), (0,)), ((), ())), preferred_element_type=jnp.float32)
        return value.astype(jnp.bfloat16).astype(jnp.float32)

    first_group = True
    for chunk in range(chunk_count):
        for group in range(own_refs[chunk].shape[0]):
            own = own_refs[chunk][group]
            turned = rotated(own)
            left = jnp.concatenate(
                [own * masks_ref[0], turned * masks_ref[1], own * masks_ref[2], turned * masks_ref[3]], axis=1
            )
            right = jnp.concatenate([own] + [near[chunk][group] for near in near_refs], axis=1)
            near = product(left, right)
            far = far_refs[chunk][group]
            first = jnp.where(lower, own, far)
            second = jnp.where(lower, far, own)
            far_left = jnp.concatenate(
                [first * masks_ref[2 * half], rotated(first) * masks_ref[2 * half + 1]], axis=1
            )
            far = product(far_left, second)
            if first_group:
                near_sum[...] = near
                far_sum[...] = far
            else:
                near_sum[...] += near
                far_sum[...] += far
            first_group = False
    for h in range(2):
        for r in range(1 + len(near_refs)):
            for p in range(2):
                start = (2 * h + p) * width
                place = (h, r, pl.ds(p, width, stride=2), slice(None))
                total = near_sum[start : start + width, r * width : (r + 1) * width]
                near_out[(slot,) + place] = total if near_before is None else total + near_before[(0,) + place]
    for p in range(2):
        place = (pl.ds(p, width, stride=2), slice(None))
        total = far_sum[p * width : (p + 1) * width, :]
        far_out[(slot,) + place] = total if far_before is None else total + far_before[(0,) + place]
    if streamed:

        def writes(g):
            return [
                pltpu.make_async_copy(near_out.at[g, 0], near_hbm.at[g, 0], sems.at[g, 0]),
                pltpu.make_async_copy(near_out.at[g, 1], near_hbm.at[g, 1], sems.at[g, 1]),
                pltpu.make_async_copy(far_out.at[g], far_hbm.at[g], sems.at[g, 2]),
            ]

        for write in writes(slot):
            write.start()

        @pl.when(slot == pl.num_programs(0) - 1)
        def _():
            for g in range(near_out.shape[0]):
                for write in writes(g):
                    write.wait()


def pair_stack(own, near, far, window_count, before=(), in_place=False, streamed=False):
    all_rows, width = own[0].shape[1:]
    rows = 4 * window_count
    per_device = all_rows // rows
    rounds = 1 + len(near)
    lower = (lax.axis_index("chan") < lax.axis_size("chan") // 2).astype(jnp.int32).reshape(1)
    index = np.arange(rows)
    part, half = index // (2 * window_count), index // window_count % 2
    sign = np.where(part == 0, 1.0, -1.0)
    masks = np.stack([half == 0, (half == 0) * sign, half == 1, (half == 1) * sign])
    masks = np.broadcast_to(masks[:, :, None], (4, rows, width)).astype(ml_dtypes.bfloat16)
    operands = [chunk for chunks in [own] + near + [far] for chunk in chunks]
    sums = [
        pl.BlockSpec((1, 2, rounds, 2 * width, width), lambda g, *_: (g, 0, 0, 0, 0)),
        pl.BlockSpec((1, 2 * width, width), lambda g, *_: (g, 0, 0)),
    ]
    return pl.pallas_call(
        functools.partial(pair_kernel, len(own), len(operands), streamed),
        grid_spec=pltpu.PrefetchScalarGridSpec(
            num_scalar_prefetch=1,
            grid=(per_device,),
            in_specs=[pl.BlockSpec((4, rows, width), lambda g, *_: (0, 0, 0))]
            + [pl.BlockSpec((chunk.shape[0], rows, width), lambda g, *_: (0, g, 0)) for chunk in operands]
            + (sums if before else []),
            out_specs=[pl.BlockSpec(memory_space=pltpu.HBM)] * 2 if streamed else sums,
            scratch_shapes=[
                pltpu.VMEM((4 * width, rounds * width), jnp.float32),
                pltpu.VMEM((2 * width, width), jnp.float32),
            ]
            + (
                [
                    pltpu.VMEM((per_device, 2, rounds, 2 * width, width), jnp.float32),
                    pltpu.VMEM((per_device, 2 * width, width), jnp.float32),
                    pltpu.SemaphoreType.DMA((per_device, 3)),
                ]
                if streamed
                else []
            ),
        ),
        out_shape=[
            jax.ShapeDtypeStruct((per_device, 2, rounds, 2 * width, width), jnp.float32),
            jax.ShapeDtypeStruct((per_device, 2 * width, width), jnp.float32),
        ],
        input_output_aliases={2 + len(operands) + i: i for i in range(len(before) if in_place else 0)},
        compiler_params=pltpu.CompilerParams(vmem_limit_bytes=VMEM_LIMIT),
        name="pair_stack",
    )(lower, jnp.asarray(masks), *operands, *before)


def shifted(value, steps):
    count = lax.axis_size("chan")
    return lax.ppermute(value, "chan", [(source, (source + steps) % count) for source in range(count)])


def swapped(value, axis, bit):
    return lax.ppermute(value, axis, [(source, source ^ bit) for source in range(lax.axis_size(axis))])


def moved(value, steps):
    count = lax.axis_size("tm")
    return lax.ppermute(value, "tm", [(source, (source + 2 * steps) % count) for source in range(count)])


def phase_kernel(kept, made, copies, *refs):
    sources, outs = refs[kept : len(refs) - kept - made], refs[len(refs) - made :]
    odd = lax.rem(lax.axis_index("chan"), 2) == 1

    def run(chosen):
        for when, source, target, first in copies:
            if when == chosen:
                outs[target][first : first + sources[source].shape[0]] = sources[source][...]

    run("always")
    if any(copy[0] != "always" for copy in copies):
        pl.when(odd)(functools.partial(run, "odd"))
        pl.when(jnp.logical_not(odd))(functools.partial(run, "even"))


def phase(kept, sources=(), counts=(), copies=()):
    made = [jax.ShapeDtypeStruct((count,) + sources[0].shape[1:], sources[0].dtype) for count in counts]
    anywhere, vmem = pl.BlockSpec(memory_space=pl.ANY), pl.BlockSpec(memory_space=pltpu.VMEM)
    return pl.pallas_call(
        functools.partial(phase_kernel, len(kept), len(made), tuple(copies)),
        in_specs=[anywhere] * len(kept) + [vmem] * len(sources),
        out_specs=[anywhere] * len(kept) + [vmem] * len(made),
        out_shape=[jax.ShapeDtypeStruct(x.shape, x.dtype) for x in kept] + made,
        input_output_aliases={i: i for i in range(len(kept))},
        compiler_params=pltpu.CompilerParams(vmem_limit_bytes=VMEM_LIMIT),
        name="phase",
    )(*kept, *sources)


def near_payload(kept, own, far):
    return phase(kept, [own, far], [own.shape[0]], [("odd", 0, 0, 0), ("even", 1, 0, 0)])


def square_stack(records):
    window_count = records.shape[0]
    count = lax.axis_size("tm")

    def target_of(place):
        me = lax.axis_index("tm")
        core = me % 2 if place < 4 else 1 - me % 2
        return (me // 2 + (1, 2, 3, 0)[place % 4]) % (count // 2) * 2 + core

    after_one, opposite, before, here, core = whiten(records, count, target_of, (1, 1, 1, 1, 4), (1, 1, 1, 1, 4))
    far_swap = functools.partial(swapped, axis="chan", bit=2)
    near_swap = functools.partial(swapped, axis="chan", bit=1)
    stack = functools.partial(pair_stack, window_count=window_count)
    grow = functools.partial(stack, in_place=True)
    token = jnp.zeros((8, 128), jnp.float32)

    after_one = moved(after_one, 1)
    core = swapped(core, "tm", 1)
    here_far = far_swap(here)
    core_after, core_last, core_before, core_here = (core[i : i + 1] for i in range(4))
    token, also, after_two, last, before_two = phase(
        [token],
        [core_here, core_after, core_last, core_before],
        [1, 1, 1, 1],
        [("always", i, i, 0) for i in range(4)],
    )
    after_two = moved(after_two, 1)
    also_far = far_swap(also)

    token, after_one, before = phase([token, after_one, before])
    before_one = moved(before, 3)

    token, here_send = near_payload([token], here, here_far)
    here_near = near_swap(here_send)

    token, after = phase([token], [after_one, after_two], [2], [("always", 0, 0, 0), ("always", 1, 0, 1)])
    after_far = far_swap(after)

    token, before_two, also_send = near_payload([token, before_two], also, also_far)
    before_two = moved(before_two, 3)
    also_near = near_swap(also_send)


    token, before_one, opposite, here_near = phase([token, before_one, opposite, here_near])
    two = moved(opposite, 2)

    token, last, also_near, before = phase([token, last, also_near], [before_one, before_two], [2], [("always", 0, 0, 0), ("always", 1, 0, 1)])
    last = moved(last, 2)
    before_far = far_swap(before)

    token, here, after_send = near_payload([token, here], after, after_far)
    after_near = near_swap(after_send)
    near_sum, far_sum = stack([here, also], [[here_near, also_near]], [here_far, also_far])

    token, far_sum, before_send = near_payload([token, far_sum], before, before_far)
    before_near = near_swap(before_send)

    token, two = phase([token, two])
    two_far = far_swap(two)

    token, two_send = near_payload([token], two, two_far)
    two_near = near_swap(two_send)

    last_near = shifted(last, -1)
    last_far = far_swap(last)
    near_sum, far_sum = grow(
        [after, before], [[after_near, before_near]], [after_far, before_far], before=(near_sum, far_sum)
    )
    return stack(
        [two, last], [[two_near, last_near]], [two_far, last_far], before=(near_sum, far_sum), streamed=True
    )


def plain_stack(records):
    count, chan_count = lax.axis_size("tm"), lax.axis_size("chan")
    whitened = whiten(records, count, lambda place: place, (count,), (count,))[0]
    own = lax.all_to_all(whitened, "tm", split_axis=0, concat_axis=0, tiled=True)
    mates = [shifted(own, -offset) for offset in range(1, chan_count // 2 + 1)]
    return pair_stack([own], [[mate] for mate in mates[:-1]], [mates[-1]], records.shape[0])


def body(records):
    width = records.shape[1]
    square = lax.axis_size("tm") == 8 and lax.axis_size("chan") == 4
    near, far = (square_stack if square else plain_stack)(records)
    near = near.reshape(near.shape[:3] + (width, 2, width))
    return near, far.reshape(far.shape[0], width, 2, width)


def solution(mesh):
    return jax.shard_map(
        body,
        mesh=mesh,
        in_specs=(P("tm", "chan", None),),
        out_specs=(P("tm", None, None, "chan", None, None), P("tm", "chan", None, None)),
        check_vma=False,
    )
```

```python
import functools
import math

import jax
import jax.numpy as jnp
import ml_dtypes
import numpy as np
from jax import lax
from jax.experimental import pallas as pl
from jax.experimental.pallas import tpu as pltpu
from jax.sharding import PartitionSpec as P

FREQS = 64
FIRST_BIN = 32
EPSILON = 1e-06
WHITEN_VMEM = 52 * 1024 * 1024
VMEM_LIMIT = 16 * 1024 * 1024


def dft_table(bins, samples):
    row = lax.broadcasted_iota(jnp.int32, (bins, samples), 0)
    position = lax.broadcasted_iota(jnp.int32, (bins, samples), 1)
    frequency = FIRST_BIN + FREQS // 2 * (row % 2) + row // 4
    phase_index = (frequency * position + samples // 4 * (row // 2 % 2)) % samples
    scale = 2.0 * math.pi / samples
    taper = 0.5 - 0.5 * jnp.cos(scale * lax.broadcasted_iota(jnp.int32, (1, samples), 1).astype(jnp.float32))
    return (taper * jnp.cos(scale * phase_index.astype(jnp.float32))).astype(jnp.bfloat16)


def whiten_kernel(scale, step_windows, counts, target_of, records_hbm, *refs):
    out_refs = refs[: len(counts)]
    table_ref, records_ref, rows_ref, record_sems = refs[len(counts) :]
    window_count, channels, samples = records_ref.shape
    bins = table_ref.shape[0]
    steps = window_count // step_windows

    def record_copy(step):
        span = pl.ds(step * step_windows, step_windows)
        return pltpu.make_async_copy(records_hbm.at[span], records_ref.at[span], record_sems.at[step])

    for step in range(min(2, steps)):
        record_copy(step).start()
    table_ref[...] = dft_table(bins, samples)
    for step in range(steps):
        record_copy(step).wait()
        if step + 2 < steps:
            record_copy(step + 2).start()
        windows = records_ref[step * step_windows : (step + 1) * step_windows]
        spectra = lax.dot_general(
            table_ref[...],
            windows.reshape(step_windows * channels, samples),
            (((1,), (1,)), ((), ())),
            preferred_element_type=jnp.float32,
        )
        mean_square = jnp.sum(spectra * spectra, axis=0, keepdims=True) * (1.0 / bins)
        whitened = spectra * (scale / jnp.sqrt(mean_square + EPSILON))
        for local in range(step_windows):
            window = step * step_windows + local
            for row in range(0, bins, 8):
                rows_ref[pl.ds(row * window_count + window, 8, stride=window_count), :] = whitened[
                    row : row + 8, local * channels : (local + 1) * channels
                ]
    place = 0
    for out_ref, count in zip(out_refs, counts):
        rows = out_ref.shape[1]
        for index in range(count):
            start = pl.multiple_of(target_of(place) * rows, 16)
            out_ref[index] = rows_ref[pl.ds(start, rows), :].astype(jnp.bfloat16)
            place += 1


def whiten(records, time_count, target_of, counts, sizes):
    window_count, channels, samples = records.shape
    step_windows = window_count // 4 if window_count % 4 == 0 else window_count
    bins = 2 * FREQS
    rows = bins * window_count // time_count
    scale = float(window_count * time_count) ** (-0.25)
    return pl.pallas_call(
        functools.partial(whiten_kernel, scale, step_windows, counts, target_of),
        in_specs=[pl.BlockSpec(memory_space=pltpu.HBM)],
        out_specs=[pl.BlockSpec(memory_space=pltpu.VMEM)] * len(sizes),
        out_shape=[jax.ShapeDtypeStruct((size, rows, channels), jnp.bfloat16) for size in sizes],
        scratch_shapes=[
            pltpu.VMEM((bins, samples), jnp.bfloat16),
            pltpu.VMEM(records.shape, jnp.bfloat16),
            pltpu.VMEM((bins * window_count, channels), jnp.float32),
            pltpu.SemaphoreType.DMA((window_count // step_windows,)),
        ],
        compiler_params=pltpu.CompilerParams(vmem_limit_bytes=WHITEN_VMEM),
        name="whiten",
    )(records)


def rotated(block):
    middle = block.shape[0] // 2
    return jnp.concatenate([block[middle:], block[:middle]], axis=0)


def product(left, right):
    value = lax.dot_general(left, right, (((0,), (0,)), ((), ())), preferred_element_type=jnp.float32)
    return value.astype(jnp.bfloat16).astype(jnp.float32)


def both_halves(own, masks_ref):
    turned = rotated(own)
    return jnp.concatenate(
        [own * masks_ref[0], turned * masks_ref[1], own * masks_ref[2], turned * masks_ref[3]], axis=1
    )


def far_product(own, far, lower, masks_ref):
    half = jnp.where(lower, 0, 1)
    first = jnp.where(lower, own, far)
    second = jnp.where(lower, far, own)
    left = jnp.concatenate([first * masks_ref[2 * half], rotated(first) * masks_ref[2 * half + 1]], axis=1)
    return product(left, second)


def pair_kernel(chunk_count, operand_count, lower_ref, masks_ref, *refs):
    near_out, far_out, near_sum, far_sum = refs[-4:]
    near_before, far_before = refs[operand_count:-4] or (None, None)
    arrays = [refs[start : start + chunk_count] for start in range(0, operand_count, chunk_count)]
    own_refs, near_refs, far_refs = arrays[0], arrays[1:-1], arrays[-1]
    width = masks_ref.shape[2]
    lower = lower_ref[0] > 0

    first_group = True
    for chunk in range(chunk_count):
        for group in range(own_refs[chunk].shape[0]):
            own = own_refs[chunk][group]
            right = jnp.concatenate([own] + [near[chunk][group] for near in near_refs], axis=1)
            near = product(both_halves(own, masks_ref), right)
            far = far_product(own, far_refs[chunk][group], lower, masks_ref)
            if first_group:
                near_sum[...] = near
                far_sum[...] = far
            else:
                near_sum[...] += near
                far_sum[...] += far
            first_group = False
    for h in range(2):
        for r in range(1 + len(near_refs)):
            for p in range(2):
                start = (2 * h + p) * width
                place = (0, h, r, pl.ds(p, width, stride=2), slice(None))
                total = near_sum[start : start + width, r * width : (r + 1) * width]
                near_out[place] = total if near_before is None else total + near_before[place]
    for p in range(2):
        place = (0, pl.ds(p, width, stride=2), slice(None))
        total = far_sum[p * width : (p + 1) * width, :]
        far_out[place] = total if far_before is None else total + far_before[place]


def last_kernel(count, finish_far, lower_ref, masks_ref, *refs):
    own_refs, mate_refs = refs[:count], refs[count : 2 * count]
    if finish_far:
        near_before, far_before, near_hbm, far_hbm, near_sum, far_sum, near_stage, far_stage, sems = refs[2 * count :]
    else:
        near_before, _, near_hbm, near_sum, near_stage, sems = refs[2 * count :]
    rows, width = masks_ref.shape[1:]
    lower = lower_ref[0] > 0
    r = 0 if finish_far else 1
    writes = []
    for g in range(near_stage.shape[0]):
        span = slice(g * rows, (g + 1) * rows)
        near_total = near_sum.at[g % 2]
        groups = [(c, i) for c in range(count) for i in range(own_refs[c].shape[0])]
        for place, (chunk, group) in enumerate(groups):
            own, mate = own_refs[chunk][group, span], mate_refs[chunk][group, span]
            near = product(both_halves(own, masks_ref), own if finish_far else mate)
            near_total[...] = near if place == 0 else near_total[...] + near
            if finish_far:
                far = far_product(own, mate, lower, masks_ref)
                far_sum[g % 2] = far if place == 0 else far_sum[g % 2] + far
        for h in range(2):
            for p in range(2):
                start = (2 * h + p) * width
                pair_rows = pl.ds(p, width, stride=2)
                near_stage[g, h, pair_rows, :] = (
                    near_total[start : start + width, :] + near_before[g, h, r, pair_rows, :]
                )
            writes.append(pltpu.make_async_copy(near_stage.at[g, h], near_hbm.at[g, h, r], sems.at[g, h]))
            writes[-1].start()
        if finish_far:
            for p in range(2):
                pair_rows = pl.ds(p, width, stride=2)
                far_stage[g, pair_rows, :] = (
                    far_sum[g % 2, p * width : (p + 1) * width, :] + far_before[g, pair_rows, :]
                )
            writes.append(pltpu.make_async_copy(far_stage.at[g], far_hbm.at[g], sems.at[g, 2]))
            writes[-1].start()
    for write in writes:
        write.wait()


def stack_tables(window_count, width):
    lower = (lax.axis_index("chan") < lax.axis_size("chan") // 2).astype(jnp.int32).reshape(1)
    index = np.arange(4 * window_count)
    part, half = index // (2 * window_count), index // window_count % 2
    sign = np.where(part == 0, 1.0, -1.0)
    masks = np.stack([half == 0, (half == 0) * sign, half == 1, (half == 1) * sign])
    masks = np.broadcast_to(masks[:, :, None], masks.shape + (width,)).astype(ml_dtypes.bfloat16)
    return lower, jnp.asarray(masks)


def last_stack(own, mates, window_count, near_before, far_before=None, near_done=None):
    per_device, _, rounds, _, width = near_before.shape
    finish_far = near_done is None
    assert rounds == 2
    vmem, hbm = pl.BlockSpec(memory_space=pltpu.VMEM), pl.BlockSpec(memory_space=pltpu.HBM)
    near_shape = jax.ShapeDtypeStruct(near_before.shape, jnp.float32)
    far_shape = jax.ShapeDtypeStruct((per_device, 2 * width, width), jnp.float32)
    near_scratch = [pltpu.VMEM((2, 4 * width, width), jnp.float32)]
    far_scratch = [pltpu.VMEM((2, 2 * width, width), jnp.float32)] if finish_far else []
    near_stage = [pltpu.VMEM((per_device, 2, 2 * width, width), jnp.float32)]
    far_stage = [pltpu.VMEM((per_device, 2 * width, width), jnp.float32)] if finish_far else []
    operands = list(own) + list(mates) + [near_before]
    return pl.pallas_call(
        functools.partial(last_kernel, len(own), finish_far),
        in_specs=[pl.BlockSpec(memory_space=pltpu.SMEM)]
        + [vmem] * (1 + len(operands))
        + [vmem if finish_far else hbm],
        out_specs=[hbm, hbm] if finish_far else hbm,
        out_shape=[near_shape, far_shape] if finish_far else near_shape,
        scratch_shapes=near_scratch
        + far_scratch
        + near_stage
        + far_stage
        + [pltpu.SemaphoreType.DMA((per_device, 3))],
        input_output_aliases={} if finish_far else {2 + len(operands): 0},
        compiler_params=pltpu.CompilerParams(vmem_limit_bytes=VMEM_LIMIT),
        name="last_stack",
    )(*stack_tables(window_count, width), *operands, far_before if finish_far else near_done)


def pair_stack(own, near, far, window_count, before=(), in_place=False):
    all_rows, width = own[0].shape[1:]
    rows = 4 * window_count
    per_device = all_rows // rows
    rounds = 1 + len(near)
    lower, masks = stack_tables(window_count, width)
    operands = [chunk for chunks in [own] + near + [far] for chunk in chunks]
    sums = [
        pl.BlockSpec((1, 2, rounds, 2 * width, width), lambda g, *_: (g, 0, 0, 0, 0)),
        pl.BlockSpec((1, 2 * width, width), lambda g, *_: (g, 0, 0)),
    ]
    blocks = [pl.BlockSpec((chunk.shape[0], rows, width), lambda g, *_: (0, g, 0)) for chunk in operands]
    return pl.pallas_call(
        functools.partial(pair_kernel, len(own), len(operands)),
        grid_spec=pltpu.PrefetchScalarGridSpec(
            num_scalar_prefetch=1,
            grid=(per_device,),
            in_specs=[pl.BlockSpec((4, rows, width), lambda g, *_: (0, 0, 0))] + blocks + (sums if before else []),
            out_specs=sums,
            scratch_shapes=[
                pltpu.VMEM((4 * width, rounds * width), jnp.float32),
                pltpu.VMEM((2 * width, width), jnp.float32),
            ],
        ),
        out_shape=[
            jax.ShapeDtypeStruct((per_device, 2, rounds, 2 * width, width), jnp.float32),
            jax.ShapeDtypeStruct((per_device, 2 * width, width), jnp.float32),
        ],
        input_output_aliases={2 + len(operands) + i: i for i in range(len(before) if in_place else 0)},
        compiler_params=pltpu.CompilerParams(vmem_limit_bytes=VMEM_LIMIT),
        name="pair_stack",
    )(lower, masks, *operands, *before)


def shifted(value, steps):
    count = lax.axis_size("chan")
    return lax.ppermute(value, "chan", [(source, (source + steps) % count) for source in range(count)])


def swapped(value, axis, bit):
    return lax.ppermute(value, axis, [(source, source ^ bit) for source in range(lax.axis_size(axis))])


def moved(value, steps):
    count = lax.axis_size("tm")
    return lax.ppermute(value, "tm", [(source, (source + 2 * steps) % count) for source in range(count)])


def phase_kernel(kept, made, copies, *refs):
    sources, outs = refs[kept : len(refs) - kept - made], refs[len(refs) - made :]
    odd = lax.rem(lax.axis_index("chan"), 2) == 1

    def run(chosen):
        for when, source, target, first in copies:
            if when == chosen:
                outs[target][first : first + sources[source].shape[0]] = sources[source][...]

    run("always")
    if any(copy[0] != "always" for copy in copies):
        pl.when(odd)(functools.partial(run, "odd"))
        pl.when(jnp.logical_not(odd))(functools.partial(run, "even"))


def phase(kept, sources=(), counts=(), copies=()):
    made = [jax.ShapeDtypeStruct((count,) + sources[0].shape[1:], sources[0].dtype) for count in counts]
    anywhere, vmem = pl.BlockSpec(memory_space=pl.ANY), pl.BlockSpec(memory_space=pltpu.VMEM)
    return pl.pallas_call(
        functools.partial(phase_kernel, len(kept), len(made), tuple(copies)),
        in_specs=[anywhere] * len(kept) + [vmem] * len(sources),
        out_specs=[anywhere] * len(kept) + [vmem] * len(made),
        out_shape=[jax.ShapeDtypeStruct(x.shape, x.dtype) for x in kept] + made,
        input_output_aliases={i: i for i in range(len(kept))},
        compiler_params=pltpu.CompilerParams(vmem_limit_bytes=VMEM_LIMIT),
        name="phase",
    )(*kept, *sources)


def near_payload(kept, own, far):
    return phase(kept, [own, far], [own.shape[0]], [("odd", 0, 0, 0), ("even", 1, 0, 0)])


def square_stack(records):
    window_count = records.shape[0]
    count = lax.axis_size("tm")

    def target_of(place):
        me = lax.axis_index("tm")
        core = me % 2 if place < 4 else 1 - me % 2
        return (me // 2 + (1, 2, 3, 0)[place % 4]) % (count // 2) * 2 + core

    after_one, opposite, before, here, core = whiten(records, count, target_of, (1, 1, 1, 1, 4), (1, 1, 1, 1, 4))
    far_swap = functools.partial(swapped, axis="chan", bit=2)
    near_swap = functools.partial(swapped, axis="chan", bit=1)
    stack = functools.partial(pair_stack, window_count=window_count)
    grow = functools.partial(stack, in_place=True)
    token = jnp.zeros((8, 128), jnp.float32)

    after_one = moved(after_one, 1)
    core = swapped(core, "tm", 1)
    here_far = far_swap(here)
    core_after, core_last, core_before, core_here = (core[i : i + 1] for i in range(4))
    token, also, after_two, last, before_two = phase(
        [token],
        [core_here, core_after, core_last, core_before],
        [1, 1, 1, 1],
        [("always", i, i, 0) for i in range(4)],
    )
    after_two = moved(after_two, 1)
    also_far = far_swap(also)

    token, after_one, before = phase([token, after_one, before])
    before_one = moved(before, 3)

    token, here_send = near_payload([token], here, here_far)
    here_near = near_swap(here_send)

    token, after = phase([token], [after_one, after_two], [2], [("always", 0, 0, 0), ("always", 1, 0, 1)])
    after_far = far_swap(after)

    token, before_two, also_send = near_payload([token, before_two], also, also_far)
    before_two = moved(before_two, 3)
    also_near = near_swap(also_send)


    token, before_one, opposite, here_near = phase([token, before_one, opposite, here_near])
    two = moved(opposite, 2)

    token, last, also_near, before = phase([token, last, also_near], [before_one, before_two], [2], [("always", 0, 0, 0), ("always", 1, 0, 1)])
    last = moved(last, 2)
    before_far = far_swap(before)

    token, here, after_send = near_payload([token, here], after, after_far)
    after_near = near_swap(after_send)
    near_sum, far_sum = stack([here, also], [[here_near, also_near]], [here_far, also_far])

    token, far_sum, before_send = near_payload([token, far_sum], before, before_far)
    before_near = near_swap(before_send)

    token, two = phase([token, two])
    two_far = far_swap(two)

    token, two_send = near_payload([token], two, two_far)
    two_near = near_swap(two_send)

    last_near = shifted(last, -1)
    last_far = far_swap(last)
    near_sum, far_sum = grow(
        [after, before], [[after_near, before_near]], [after_far, before_far], before=(near_sum, far_sum)
    )
    near_done, far_done = last_stack([two, last], [two_far, last_far], window_count, near_sum, far_before=far_sum)
    near_done = last_stack([two, last], [two_near, last_near], window_count, near_sum, near_done=near_done)
    return near_done, far_done


def plain_stack(records):
    count, chan_count = lax.axis_size("tm"), lax.axis_size("chan")
    whitened = whiten(records, count, lambda place: place, (count,), (count,))[0]
    own = lax.all_to_all(whitened, "tm", split_axis=0, concat_axis=0, tiled=True)
    mates = [shifted(own, -offset) for offset in range(1, chan_count // 2 + 1)]
    return pair_stack([own], [[mate] for mate in mates[:-1]], [mates[-1]], records.shape[0])


def body(records):
    width = records.shape[1]
    square = lax.axis_size("tm") == 8 and lax.axis_size("chan") == 4
    near, far = (square_stack if square else plain_stack)(records)
    near = near.reshape(near.shape[:3] + (width, 2, width))
    return near, far.reshape(far.shape[0], width, 2, width)


def solution(mesh):
    return jax.shard_map(
        body,
        mesh=mesh,
        in_specs=(P("tm", "chan", None),),
        out_specs=(P("tm", None, None, "chan", None, None), P("tm", "chan", None, None)),
        check_vma=False,
    )
```

```python
import functools
import math

import jax
import jax.numpy as jnp
import ml_dtypes
import numpy as np
from jax import lax
from jax.experimental import pallas as pl
from jax.experimental.pallas import tpu as pltpu
from jax.sharding import PartitionSpec as P

FREQS = 64
FIRST_BIN = 32
EPSILON = 1e-06
WHITEN_VMEM = 52 * 1024 * 1024
VMEM_LIMIT = 16 * 1024 * 1024


def dft_table(bins, samples):
    row = lax.broadcasted_iota(jnp.int32, (bins, samples), 0)
    position = lax.broadcasted_iota(jnp.int32, (bins, samples), 1)
    frequency = FIRST_BIN + FREQS // 2 * (row % 2) + row // 4
    phase_index = (frequency * position + samples // 4 * (row // 2 % 2)) % samples
    scale = 2.0 * math.pi / samples
    taper = 0.5 - 0.5 * jnp.cos(scale * lax.broadcasted_iota(jnp.int32, (1, samples), 1).astype(jnp.float32))
    return (taper * jnp.cos(scale * phase_index.astype(jnp.float32))).astype(jnp.bfloat16)


def whiten_kernel(scale, step_windows, counts, target_of, records_hbm, *refs):
    out_refs = refs[: len(counts)]
    table_ref, records_ref, rows_ref, record_sems = refs[len(counts) :]
    window_count, channels, samples = records_ref.shape
    bins = table_ref.shape[0]
    steps = window_count // step_windows

    def record_copy(step):
        span = pl.ds(step * step_windows, step_windows)
        return pltpu.make_async_copy(records_hbm.at[span], records_ref.at[span], record_sems.at[step])

    for step in range(min(2, steps)):
        record_copy(step).start()
    table_ref[...] = dft_table(bins, samples)
    for step in range(steps):
        record_copy(step).wait()
        if step + 2 < steps:
            record_copy(step + 2).start()
        for window in range(step * step_windows, (step + 1) * step_windows):
            spectra = lax.dot_general(
                table_ref[...], records_ref[window], (((1,), (1,)), ((), ())), preferred_element_type=jnp.float32
            )
            mean_square = jnp.sum(spectra * spectra, axis=0, keepdims=True) * (1.0 / bins)
            whitened = spectra * (scale / jnp.sqrt(mean_square + EPSILON))
            for row in range(0, bins, 8):
                rows_ref[pl.ds(row * window_count + window, 8, stride=window_count), :] = whitened[row : row + 8]
    place = 0
    for out_ref, count in zip(out_refs, counts):
        rows = out_ref.shape[1]
        for index in range(count):
            start = pl.multiple_of(target_of(place) * rows, 16)
            out_ref[index] = rows_ref[pl.ds(start, rows), :].astype(jnp.bfloat16)
            place += 1


def whiten(records, time_count, target_of, counts, sizes):
    window_count, channels, samples = records.shape
    step_windows = window_count // 4 if window_count % 4 == 0 else window_count
    bins = 2 * FREQS
    rows = bins * window_count // time_count
    scale = float(window_count * time_count) ** (-0.25)
    return pl.pallas_call(
        functools.partial(whiten_kernel, scale, step_windows, counts, target_of),
        in_specs=[pl.BlockSpec(memory_space=pltpu.HBM)],
        out_specs=[pl.BlockSpec(memory_space=pltpu.VMEM)] * len(sizes),
        out_shape=[jax.ShapeDtypeStruct((size, rows, channels), jnp.bfloat16) for size in sizes],
        scratch_shapes=[
            pltpu.VMEM((bins, samples), jnp.bfloat16),
            pltpu.VMEM(records.shape, jnp.bfloat16),
            pltpu.VMEM((bins * window_count, channels), jnp.float32),
            pltpu.SemaphoreType.DMA((window_count // step_windows,)),
        ],
        compiler_params=pltpu.CompilerParams(vmem_limit_bytes=WHITEN_VMEM),
        name="whiten",
    )(records)


def rotated(block):
    middle = block.shape[0] // 2
    return jnp.concatenate([block[middle:], block[:middle]], axis=0)


def product(left, right):
    value = lax.dot_general(left, right, (((0,), (0,)), ((), ())), preferred_element_type=jnp.float32)
    return value.astype(jnp.bfloat16).astype(jnp.float32)


def both_halves(own, masks_ref):
    turned = rotated(own)
    return jnp.concatenate(
        [own * masks_ref[0], turned * masks_ref[1], own * masks_ref[2], turned * masks_ref[3]], axis=1
    )


def far_product(own, far, lower, masks_ref):
    half = jnp.where(lower, 0, 1)
    first = jnp.where(lower, own, far)
    second = jnp.where(lower, far, own)
    left = jnp.concatenate([first * masks_ref[2 * half], rotated(first) * masks_ref[2 * half + 1]], axis=1)
    return product(left, second)


def pair_kernel(chunk_count, operand_count, lower_ref, masks_ref, *refs):
    near_out, far_out, near_sum, far_sum = refs[-4:]
    near_before, far_before = refs[operand_count:-4] or (None, None)
    arrays = [refs[start : start + chunk_count] for start in range(0, operand_count, chunk_count)]
    own_refs, near_refs, far_refs = arrays[0], arrays[1:-1], arrays[-1]
    width = masks_ref.shape[2]
    lower = lower_ref[0] > 0

    first_group = True
    for chunk in range(chunk_count):
        for group in range(own_refs[chunk].shape[0]):
            own = own_refs[chunk][group]
            right = jnp.concatenate([own] + [near[chunk][group] for near in near_refs], axis=1)
            near = product(both_halves(own, masks_ref), right)
            far = far_product(own, far_refs[chunk][group], lower, masks_ref)
            if first_group:
                near_sum[...] = near
                far_sum[...] = far
            else:
                near_sum[...] += near
                far_sum[...] += far
            first_group = False
    for h in range(2):
        for r in range(1 + len(near_refs)):
            for p in range(2):
                start = (2 * h + p) * width
                place = (0, h, r, pl.ds(p, width, stride=2), slice(None))
                total = near_sum[start : start + width, r * width : (r + 1) * width]
                near_out[place] = total if near_before is None else total + near_before[place]
    for p in range(2):
        place = (0, pl.ds(p, width, stride=2), slice(None))
        total = far_sum[p * width : (p + 1) * width, :]
        far_out[place] = total if far_before is None else total + far_before[place]


def last_kernel(count, finish_far, lower_ref, masks_ref, *refs):
    own_refs, mate_refs = refs[:count], refs[count : 2 * count]
    if finish_far:
        near_before, far_before, near_hbm, far_hbm, near_sum, far_sum, near_stage, far_stage, sems = refs[2 * count :]
    else:
        near_before, _, near_hbm, near_sum, near_stage, sems = refs[2 * count :]
    rows, width = masks_ref.shape[1:]
    lower = lower_ref[0] > 0
    r = 0 if finish_far else 1
    writes = []
    for g in range(near_stage.shape[0]):
        span = slice(g * rows, (g + 1) * rows)
        near_total = near_sum.at[g % 2]
        groups = [(c, i) for c in range(count) for i in range(own_refs[c].shape[0])]
        for place, (chunk, group) in enumerate(groups):
            own, mate = own_refs[chunk][group, span], mate_refs[chunk][group, span]
            near = product(both_halves(own, masks_ref), own if finish_far else mate)
            near_total[...] = near if place == 0 else near_total[...] + near
            if finish_far:
                far = far_product(own, mate, lower, masks_ref)
                far_sum[g % 2] = far if place == 0 else far_sum[g % 2] + far
        for h in range(2):
            for p in range(2):
                start = (2 * h + p) * width
                pair_rows = pl.ds(p, width, stride=2)
                near_stage[g, h, pair_rows, :] = (
                    near_total[start : start + width, :] + near_before[g, h, r, pair_rows, :]
                )
            writes.append(pltpu.make_async_copy(near_stage.at[g, h], near_hbm.at[g, h, r], sems.at[g, h]))
            writes[-1].start()
        if finish_far:
            for p in range(2):
                pair_rows = pl.ds(p, width, stride=2)
                far_stage[g, pair_rows, :] = (
                    far_sum[g % 2, p * width : (p + 1) * width, :] + far_before[g, pair_rows, :]
                )
            writes.append(pltpu.make_async_copy(far_stage.at[g], far_hbm.at[g], sems.at[g, 2]))
            writes[-1].start()
    for write in writes:
        write.wait()


def stack_tables(window_count, width):
    lower = (lax.axis_index("chan") < lax.axis_size("chan") // 2).astype(jnp.int32).reshape(1)
    index = np.arange(4 * window_count)
    part, half = index // (2 * window_count), index // window_count % 2
    sign = np.where(part == 0, 1.0, -1.0)
    masks = np.stack([half == 0, (half == 0) * sign, half == 1, (half == 1) * sign])
    masks = np.broadcast_to(masks[:, :, None], masks.shape + (width,)).astype(ml_dtypes.bfloat16)
    return lower, jnp.asarray(masks)


def last_stack(own, mates, window_count, near_before, far_before=None, near_done=None):
    per_device, _, rounds, _, width = near_before.shape
    finish_far = near_done is None
    assert rounds == 2
    vmem, hbm = pl.BlockSpec(memory_space=pltpu.VMEM), pl.BlockSpec(memory_space=pltpu.HBM)
    near_shape = jax.ShapeDtypeStruct(near_before.shape, jnp.float32)
    far_shape = jax.ShapeDtypeStruct((per_device, 2 * width, width), jnp.float32)
    near_scratch = [pltpu.VMEM((2, 4 * width, width), jnp.float32)]
    far_scratch = [pltpu.VMEM((2, 2 * width, width), jnp.float32)] if finish_far else []
    near_stage = [pltpu.VMEM((per_device, 2, 2 * width, width), jnp.float32)]
    far_stage = [pltpu.VMEM((per_device, 2 * width, width), jnp.float32)] if finish_far else []
    operands = list(own) + list(mates) + [near_before]
    return pl.pallas_call(
        functools.partial(last_kernel, len(own), finish_far),
        in_specs=[pl.BlockSpec(memory_space=pltpu.SMEM)]
        + [vmem] * (1 + len(operands))
        + [vmem if finish_far else hbm],
        out_specs=[hbm, hbm] if finish_far else hbm,
        out_shape=[near_shape, far_shape] if finish_far else near_shape,
        scratch_shapes=near_scratch
        + far_scratch
        + near_stage
        + far_stage
        + [pltpu.SemaphoreType.DMA((per_device, 3))],
        input_output_aliases={} if finish_far else {2 + len(operands): 0},
        compiler_params=pltpu.CompilerParams(vmem_limit_bytes=VMEM_LIMIT),
        name="last_stack",
    )(*stack_tables(window_count, width), *operands, far_before if finish_far else near_done)


def pair_stack(own, near, far, window_count, before=(), in_place=False):
    all_rows, width = own[0].shape[1:]
    rows = 4 * window_count
    per_device = all_rows // rows
    rounds = 1 + len(near)
    lower, masks = stack_tables(window_count, width)
    operands = [chunk for chunks in [own] + near + [far] for chunk in chunks]
    sums = [
        pl.BlockSpec((1, 2, rounds, 2 * width, width), lambda g, *_: (g, 0, 0, 0, 0)),
        pl.BlockSpec((1, 2 * width, width), lambda g, *_: (g, 0, 0)),
    ]
    blocks = [pl.BlockSpec((chunk.shape[0], rows, width), lambda g, *_: (0, g, 0)) for chunk in operands]
    return pl.pallas_call(
        functools.partial(pair_kernel, len(own), len(operands)),
        grid_spec=pltpu.PrefetchScalarGridSpec(
            num_scalar_prefetch=1,
            grid=(per_device,),
            in_specs=[pl.BlockSpec((4, rows, width), lambda g, *_: (0, 0, 0))] + blocks + (sums if before else []),
            out_specs=sums,
            scratch_shapes=[
                pltpu.VMEM((4 * width, rounds * width), jnp.float32),
                pltpu.VMEM((2 * width, width), jnp.float32),
            ],
        ),
        out_shape=[
            jax.ShapeDtypeStruct((per_device, 2, rounds, 2 * width, width), jnp.float32),
            jax.ShapeDtypeStruct((per_device, 2 * width, width), jnp.float32),
        ],
        input_output_aliases={2 + len(operands) + i: i for i in range(len(before) if in_place else 0)},
        compiler_params=pltpu.CompilerParams(vmem_limit_bytes=VMEM_LIMIT),
        name="pair_stack",
    )(lower, masks, *operands, *before)


def shifted(value, steps):
    count = lax.axis_size("chan")
    return lax.ppermute(value, "chan", [(source, (source + steps) % count) for source in range(count)])


def swapped(value, axis, bit):
    return lax.ppermute(value, axis, [(source, source ^ bit) for source in range(lax.axis_size(axis))])


def moved(value, steps):
    count = lax.axis_size("tm")
    return lax.ppermute(value, "tm", [(source, (source + 2 * steps) % count) for source in range(count)])


def phase_kernel(kept, made, copies, *refs):
    sources, outs = refs[kept : len(refs) - kept - made], refs[len(refs) - made :]
    odd = lax.rem(lax.axis_index("chan"), 2) == 1

    def run(chosen):
        for when, source, target, first in copies:
            if when == chosen:
                outs[target][first : first + sources[source].shape[0]] = sources[source][...]

    run("always")
    if any(copy[0] != "always" for copy in copies):
        pl.when(odd)(functools.partial(run, "odd"))
        pl.when(jnp.logical_not(odd))(functools.partial(run, "even"))


def phase(kept, sources=(), counts=(), copies=()):
    made = [jax.ShapeDtypeStruct((count,) + sources[0].shape[1:], sources[0].dtype) for count in counts]
    anywhere, vmem = pl.BlockSpec(memory_space=pl.ANY), pl.BlockSpec(memory_space=pltpu.VMEM)
    return pl.pallas_call(
        functools.partial(phase_kernel, len(kept), len(made), tuple(copies)),
        in_specs=[anywhere] * len(kept) + [vmem] * len(sources),
        out_specs=[anywhere] * len(kept) + [vmem] * len(made),
        out_shape=[jax.ShapeDtypeStruct(x.shape, x.dtype) for x in kept] + made,
        input_output_aliases={i: i for i in range(len(kept))},
        compiler_params=pltpu.CompilerParams(vmem_limit_bytes=VMEM_LIMIT),
        name="phase",
    )(*kept, *sources)


def near_payload(kept, own, far):
    return phase(kept, [own, far], [own.shape[0]], [("odd", 0, 0, 0), ("even", 1, 0, 0)])


def square_stack(records):
    window_count = records.shape[0]
    count = lax.axis_size("tm")

    def target_of(place):
        me = lax.axis_index("tm")
        core = me % 2 if place < 4 else 1 - me % 2
        return (me // 2 + (1, 2, 3, 0)[place % 4]) % (count // 2) * 2 + core

    after_one, opposite, before, here, core = whiten(records, count, target_of, (1, 1, 1, 1, 4), (1, 1, 1, 1, 4))
    far_swap = functools.partial(swapped, axis="chan", bit=2)
    near_swap = functools.partial(swapped, axis="chan", bit=1)
    stack = functools.partial(pair_stack, window_count=window_count)
    grow = functools.partial(stack, in_place=True)
    token = jnp.zeros((8, 128), jnp.float32)

    after_one = moved(after_one, 1)
    core = swapped(core, "tm", 1)
    here_far = far_swap(here)
    core_after, core_last, core_before, core_here = (core[i : i + 1] for i in range(4))
    token, also, after_two, last, before_two = phase(
        [token],
        [core_here, core_after, core_last, core_before],
        [1, 1, 1, 1],
        [("always", i, i, 0) for i in range(4)],
    )
    after_two = moved(after_two, 1)
    also_far = far_swap(also)

    token, after_one, before = phase([token, after_one, before])
    before_one = moved(before, 3)

    token, here_send = near_payload([token], here, here_far)
    here_near = near_swap(here_send)

    token, after = phase([token], [after_one, after_two], [2], [("always", 0, 0, 0), ("always", 1, 0, 1)])
    after_far = far_swap(after)

    token, before_two, also_send = near_payload([token, before_two], also, also_far)
    before_two = moved(before_two, 3)
    also_near = near_swap(also_send)


    token, before_one, opposite, here_near = phase([token, before_one, opposite, here_near])
    two = moved(opposite, 2)

    token, last, also_near, before = phase([token, last, also_near], [before_one, before_two], [2], [("always", 0, 0, 0), ("always", 1, 0, 1)])
    last = moved(last, 2)
    before_far = far_swap(before)

    token, here, after_send = near_payload([token, here], after, after_far)
    after_near = near_swap(after_send)
    near_sum, far_sum = stack([here, also], [[here_near, also_near]], [here_far, also_far])

    token, far_sum, before_send = near_payload([token, far_sum], before, before_far)
    before_near = near_swap(before_send)

    token, two = phase([token, two])
    two_far = far_swap(two)

    token, two_send = near_payload([token], two, two_far)
    two_near = near_swap(two_send)

    last_near = shifted(last, -1)
    last_far = far_swap(last)
    near_sum, far_sum = grow(
        [after, before], [[after_near, before_near]], [after_far, before_far], before=(near_sum, far_sum)
    )
    near_done, far_done = last_stack([two, last], [two_far, last_far], window_count, near_sum, far_before=far_sum)
    near_done = last_stack([two, last], [two_near, last_near], window_count, near_sum, near_done=near_done)
    return near_done, far_done


def plain_stack(records):
    count, chan_count = lax.axis_size("tm"), lax.axis_size("chan")
    whitened = whiten(records, count, lambda place: place, (count,), (count,))[0]
    own = lax.all_to_all(whitened, "tm", split_axis=0, concat_axis=0, tiled=True)
    mates = [shifted(own, -offset) for offset in range(1, chan_count // 2 + 1)]
    return pair_stack([own], [[mate] for mate in mates[:-1]], [mates[-1]], records.shape[0])


def body(records):
    width = records.shape[1]
    square = lax.axis_size("tm") == 8 and lax.axis_size("chan") == 4
    near, far = (square_stack if square else plain_stack)(records)
    near = near.reshape(near.shape[:3] + (width, 2, width))
    return near, far.reshape(far.shape[0], width, 2, width)


def solution(mesh):
    return jax.shard_map(
        body,
        mesh=mesh,
        in_specs=(P("tm", "chan", None),),
        out_specs=(P("tm", None, None, "chan", None, None), P("tm", "chan", None, None)),
        check_vma=False,
    )
```
